32 devices in a mesh: groups: 2 (over y), row: 4 (over z), col: 4 (over x, core).
Axes of the slice: x: 2, y: 2, z: 4, core: 2. Of those that a mesh axis runs over, the one named last changes fastest.
Arguments:
- up_a: bfloat16 [4, 4096, 14336], P('groups', 'col', 'row'), parts along dimension 0, may hold values from -2 to 2
- up_b: bfloat16 [4, 4096, 14336], P('groups', ('row', 'col')), parts along dimension 0, may hold values from -2 to 2
- residual_perm: int32 [28672], P('groups'), parts along dimension 0, may hold values from 0 to 14335, each once
- pair_index: int32 [2], P('groups'), parts along dimension 0, may hold values from 0 to 1
Outputs:
- cost: float32 [28672, 14336], P(('groups', 'row'), 'col'), parts along dimension 0
The draws below stay inside these ranges and needn't reach their ends.
There are 2 independent parts, one for each index of `groups`. The reference program is written for one: setup_inputs(seed, part) draws one part's arguments, and reference() takes and returns one part's arrays. A program takes and returns all parts, laid end to end along the dimension named above; each array names one. Nothing has to cross between parts.
Inputs may be any that keep to these rules, and one draw needn't show every extreme that they name: `residual_perm`: each unit of model B appears exactly once.
All inputs are finite; a program needn't handle non-finite values.
Results may differ from the reference program's by a relative error of at most 0.0003.
Values may be sent and summed in bfloat16 or wider, within the bound.
No kernel may reach another device: no remote copies, remote signals or barrier semaphores. Data moves between devices by JAX's collectives and lax.ppermute only.
A program may use at most 320 MiB of HBM per device.

```python
import jax
import jax.numpy as jnp
from jax import lax

FFW = 14336
LAYERS = 2
KW = 4096


def block_scale(key, shape, pieces, least, high):
    gain = 1.0
    for axis_at, shards_of in pieces:
        draws = jax.random.uniform(jax.random.fold_in(jax.random.fold_in(key, 6), axis_at), (shards_of,), jnp.float32, least / len(pieces), high / len(pieces))
        gain = gain * jnp.repeat(jnp.exp(draws), shape[axis_at] // shards_of).reshape((-1,) + (1,) * (len(shape) - 1 - axis_at))
    return gain


def noise(rng, shape, scale, most, cuts=(), kind=jnp.bfloat16):
    drawn = scale * jax.random.normal(rng, shape, jnp.float32)
    if cuts:
        drawn = drawn * block_scale(rng, shape, cuts, -0.22, 0.18)
    return jnp.clip(drawn, -most, most).astype(kind)


def setup_inputs(seed: int = 0, part: int = 0) -> dict:
    splits = jax.random.split(jax.random.key(seed), 5)
    part_keys = jax.random.split(jax.random.fold_in(splits[4], part), 5)
    return {
        "up_a": noise(part_keys[0], (LAYERS, KW, FFW), 0.15, 2.0, ((1, 4), (2, 4))),
        "up_b": noise(part_keys[1], (LAYERS, KW, FFW), 0.15, 2.0, ((1, 16),)),
        "residual_perm": jax.random.permutation(part_keys[2], FFW).astype(jnp.int32),
        "pair_index": jax.random.randint(part_keys[3], (1,), 0, LAYERS).astype(jnp.int32),
    }


def reference(up_a, up_b, residual_perm, pair_index):
    layer = pair_index[0]
    left_units = lax.dynamic_index_in_dim(up_a, layer, 0, keepdims=False)
    right_units = lax.dynamic_index_in_dim(up_b, layer, 0, keepdims=False)
    permuted_up = jnp.take(right_units, residual_perm, axis=1)
    return jnp.dot(left_units.T, permuted_up, preferred_element_type=jnp.float32)
```

```python
import functools

import jax
import jax.numpy as jnp
from jax import lax
from jax.experimental import pallas as pl
from jax.experimental.pallas import tpu as pltpu
from jax.sharding import PartitionSpec as P

LANES = 128
VMEM_LIMIT = 52 * 2**20
WIDTHS = (2, 2, 4, 4, 4, 4, 4, 2, 2)


def widths_of(positions):
    units = positions // LANES
    parts = WIDTHS if sum(WIDTHS) == units else (1,) * units
    return [part * LANES for part in parts]


def select_kernel(slots, layer_ref, units_ref, perm_ref, *refs):
    outs, hot = refs[:slots], refs[slots]
    units = units_ref.shape[2]
    width = outs[0].shape[1]
    step = 1024 if units % 1024 == 0 else units
    for slot in range(slots):
        for start in range(0, width, 256):
            size = min(256, width - start)
            wanted = perm_ref[slot : slot + 1, start : start + size]
            for at in range(0, units, step):
                index = lax.broadcasted_iota(jnp.int32, (step, size), 0) + at
                hot[at : at + step, :size] = jnp.where(index == wanted, 1.0, 0.0).astype(jnp.bfloat16)
            outs[slot][:, start : start + size] = jnp.dot(
                units_ref[0], hot[:, :size], preferred_element_type=jnp.float32
            ).astype(jnp.bfloat16)


def select_units(up_b, layer, perms, width):
    slots = perms.shape[0]
    _, features, units = up_b.shape
    return pl.pallas_call(
        functools.partial(select_kernel, slots),
        out_shape=[jax.ShapeDtypeStruct((features, width), jnp.bfloat16)] * slots,
        grid_spec=pltpu.PrefetchScalarGridSpec(
            num_scalar_prefetch=1,
            grid=(1,),
            in_specs=[
                pl.BlockSpec((1, features, units), lambda i, layer: (layer[0], 0, 0)),
                pl.BlockSpec((slots, width), lambda i, layer: (0, 0)),
            ],
            out_specs=[pl.BlockSpec((features, width), lambda i, layer: (0, 0))] * slots,
            scratch_shapes=[pltpu.VMEM((units, 256), jnp.bfloat16)],
        ),
        compiler_params=pltpu.CompilerParams(vmem_limit_bytes=VMEM_LIMIT),
        cost_estimate=pl.CostEstimate(
            flops=2 * features * units * width * slots,
            bytes_accessed=2 * features * (units + width * slots),
            transcendentals=0,
        ),
        name="select_units",
    )(layer, up_b, perms)


def place_kernel(slots, at_ref, *refs):
    out = refs[slots]
    for slot in range(slots):
        out[at_ref[slot]] = refs[slot][...]


def place(at, blocks):
    slots = len(blocks)
    features, width = blocks[0].shape
    whole = pl.BlockSpec((features, width), lambda i, at: (0, 0))
    return pl.pallas_call(
        functools.partial(place_kernel, slots),
        out_shape=jax.ShapeDtypeStruct((slots, features, width), jnp.bfloat16),
        grid_spec=pltpu.PrefetchScalarGridSpec(
            num_scalar_prefetch=1,
            grid=(1,),
            in_specs=[whole] * slots,
            out_specs=pl.BlockSpec((slots, features, width), lambda i, at: (0, 0, 0)),
        ),
        compiler_params=pltpu.CompilerParams(vmem_limit_bytes=VMEM_LIMIT),
        cost_estimate=pl.CostEstimate(
            flops=0, bytes_accessed=4 * slots * features * width, transcendentals=0
        ),
        name="place",
    )(at, *blocks).reshape(slots * features, width)


def turn_kernel(layer_ref, units_ref, after_ref, out_ref):
    out_ref[...] = units_ref[0].T


def turn(up_a, layer, after):
    _, features, units = up_a.shape
    tile = 512 if units % 512 == 0 else 256
    return pl.pallas_call(
        turn_kernel,
        out_shape=jax.ShapeDtypeStruct((units, features), jnp.bfloat16),
        grid_spec=pltpu.PrefetchScalarGridSpec(
            num_scalar_prefetch=1,
            grid=(units // tile,),
            in_specs=[
                pl.BlockSpec((1, features, tile), lambda i, layer: (layer[0], 0, i)),
                pl.BlockSpec(memory_space=pl.ANY),
            ],
            out_specs=pl.BlockSpec((tile, features), lambda i, layer: (i, 0)),
        ),
        compiler_params=pltpu.CompilerParams(vmem_limit_bytes=VMEM_LIMIT),
        cost_estimate=pl.CostEstimate(
            flops=0, bytes_accessed=4 * features * units, transcendentals=0
        ),
        name="turn",
    )(layer, up_a, after)


def product_kernel(pieces, blocks, places, at_ref, *refs):
    lefts, rights, out = refs[:pieces], refs[pieces : pieces + blocks], refs[-1]
    depth = lefts[0].shape[2]
    total = None
    for piece, (block, row) in enumerate(places):
        term = jnp.dot(
            lefts[piece][0],
            rights[block][row : row + depth, :],
            preferred_element_type=jnp.float32,
        )
        total = term if total is None else total + term
    out[...] = total


def product(left, at, rights, cost, offset, positions):
    shares, units, share = left.shape
    blocks = len(rights)
    block, width = rights[0].shape
    depth = min(share, block)
    per_block = block // depth
    tile = 512 if units % 512 == 0 else 256
    column = offset // width
    places = [(k, t * depth) for k in range(blocks) for t in range(per_block)]

    def left_at(k, row, i, at):
        feature = at[k] * block + row
        return (feature // share, i, (feature % share) // depth)

    in_specs = [
        pl.BlockSpec((1, tile, depth), functools.partial(left_at, k, row)) for k, row in places
    ] + [pl.BlockSpec((block, width), lambda i, at: (0, 0))] * blocks
    operands = [left] * len(places) + list(rights)
    aliases = {}
    if cost is not None:
        in_specs.append(pl.BlockSpec(memory_space=pl.ANY))
        operands.append(cost)
        aliases = {len(operands): 0}
    return pl.pallas_call(
        functools.partial(product_kernel, len(places), blocks, places),
        out_shape=jax.ShapeDtypeStruct((units, positions), jnp.float32),
        grid_spec=pltpu.PrefetchScalarGridSpec(
            num_scalar_prefetch=1,
            grid=(units // tile,),
            in_specs=in_specs,
            out_specs=pl.BlockSpec((tile, width), lambda i, at: (i, column)),
        ),
        input_output_aliases=aliases,
        compiler_params=pltpu.CompilerParams(vmem_limit_bytes=VMEM_LIMIT),
        cost_estimate=pl.CostEstimate(
            flops=2 * units * width * block * blocks,
            bytes_accessed=2 * shares * share * units + 2 * block * blocks * width + 4 * units * width,
            transcendentals=0,
        ),
        name="product",
    )(at, *operands)


def exchange(sent, cols):
    back = [sent[0]]
    for s in range(1, cols):
        if cols & (cols - 1) == 0:
            pairs = [(i, i ^ s) for i in range(cols)]
        else:
            pairs = [(i, (i + s) % cols) for i in range(cols)]
        back.append(lax.ppermute(sent[s], "col", pairs))
    return back


def gather_rows(own, rows):
    if rows != 4:
        shifted = [
            lax.ppermute(own, "row", [(i, (i + s) % rows) for i in range(rows)])
            for s in range(1, rows)
        ]
        return [own] + shifted
    ahead = lax.ppermute(own, "row", [(0, 1), (1, 2), (2, 3), (3, 0)])
    behind = lax.ppermute(own, "row", [(1, 0), (2, 1), (3, 2), (0, 3)])
    onward = lax.select(lax.axis_index("row") % 2 == 1, behind, ahead)
    across = lax.ppermute(onward, "row", [(0, 1), (1, 0), (2, 3), (3, 2)])
    return [own, ahead, across, behind]


def solution(mesh):
    rows, cols = mesh.shape["row"], mesh.shape["col"]

    def shards(up_a, up_b, residual_perm, pair_index):
        r, c = lax.axis_index("row"), lax.axis_index("col")
        layer = pair_index
        positions = residual_perm.shape[0] // cols
        steps = jnp.arange(cols, dtype=jnp.int32)
        if cols & (cols - 1) == 0:
            to, come = c ^ steps, c ^ steps
        else:
            to, come = (c + steps) % cols, (c - steps) % cols
        perms = jnp.take(residual_perm.reshape(cols, positions), to, axis=0)
        at = (r - jnp.arange(rows, dtype=jnp.int32)) % rows

        left, cost, offset = None, None, 0
        for width in widths_of(positions):
            wanted = lax.slice_in_dim(perms, offset, offset + width, axis=1)
            back = exchange(select_units(up_b, layer, wanted, width), cols)
            own = place(come, back)
            if left is None:
                left = lax.all_gather(turn(up_a, layer, own), "col", axis=0)
            cost = product(left, at, gather_rows(own, rows), cost, offset, positions)
            offset += width
        return cost

    placed = (
        P("groups", "col", "row"),
        P("groups", ("row", "col"), None),
        P("groups"),
        P("groups"),
    )
    return jax.shard_map(
        shards, mesh=mesh, in_specs=placed, out_specs=P(("groups", "row"), "col"), check_vma=False
    )
```

```python
import functools

import jax
import jax.numpy as jnp
from jax import lax
from jax.experimental import pallas as pl
from jax.experimental.pallas import tpu as pltpu
from jax.sharding import PartitionSpec as P

LANES = 128
VMEM_LIMIT = 52 * 2**20


def taking(us):
    return pl.CostEstimate(flops=int(us * 0.3 * 1.15e9), bytes_accessed=0, transcendentals=0)
WIDTHS = (4, 4, 4, 4, 4, 4, 2, 2)
ORDER = (
    "S0 A0 L0 S1",
    "S2 L1 O0 S3",
    "L2 O1 S4 W0.2",
    "L3 O2 S5 W1.2",
    "L4 X0 O3 S6",
    "W2.2 L5 X1 O4",
    "X2 W3.2 L6 O5",
    "X3 W4.2 O6 X4",
    "W5.2 L7 X5 O7",
    "X6 X7",
)
TOGETHER = {6: 2}


def plan(positions, rows):
    units = positions // LANES
    if sum(WIDTHS) == units and rows == 4:
        steps = " ".join(ORDER).split()
        order = [(step[0], step[1:]) for step in steps]
        return [part * LANES for part in WIDTHS], order, TOGETHER
    steps = [(kind, str(p)) for p in range(units) for kind in "SLX"]
    if rows == 4:
        steps = [(kind, str(p)) for p in range(units) for kind in "SLOX"]
    return [LANES] * units, steps[:2] + [("A", "0")] + steps[2:], {}


def select_kernel(slots, offset, layer_ref, to_ref, units_ref, perm_ref, *refs):
    outs, held = refs[-slots - 1 : -1], refs[-1]
    units = units_ref.shape[2]
    width = outs[0].shape[1]
    tile = 256 if width % 256 == 0 else width
    tiles = width // tile
    step = 1024 if units % 1024 == 0 else units

    @pl.loop(0, slots * tiles)
    def _(part):
        slot, start = part // tiles, pl.multiple_of((part % tiles) * tile, tile)
        wanted = perm_ref[to_ref[slot], :, pl.ds(pl.multiple_of(offset + start, LANES), tile)]

        total = None
        for at in range(0, units, step):
            index = lax.broadcasted_iota(jnp.int32, (step, tile), 0) + at
            hot = jnp.where(index == wanted, 1.0, 0.0).astype(jnp.bfloat16)
            term = jnp.dot(
                units_ref[0, :, at : at + step], hot, preferred_element_type=jnp.float32
            )
            total = term if total is None else total + term
        held[slot, :, pl.ds(start, tile)] = total.astype(jnp.bfloat16)

    for slot in range(slots):
        outs[slot][...] = held[slot]


def select_units(up_b, layer, perm, to, offset, width, after):
    slots, _, positions = perm.shape
    _, features, units = up_b.shape
    return pl.pallas_call(
        functools.partial(select_kernel, slots, offset),
        out_shape=[jax.ShapeDtypeStruct((features, width), jnp.bfloat16)] * slots,
        grid_spec=pltpu.PrefetchScalarGridSpec(
            num_scalar_prefetch=2,
            grid=(1,),
            in_specs=[
                pl.BlockSpec((1, features, units), lambda i, layer, to: (layer[0], 0, 0)),
                pl.BlockSpec((slots, 1, positions), lambda i, layer, to: (0, 0, 0)),
            ]
            + [pl.BlockSpec(memory_space=pl.ANY)] * len(after),
            out_specs=[pl.BlockSpec((features, width), lambda i, layer, to: (0, 0))] * slots,
            scratch_shapes=[
                pltpu.VMEM((slots, features, width), jnp.bfloat16),
            ],
        ),
        compiler_params=pltpu.CompilerParams(vmem_limit_bytes=VMEM_LIMIT),
        cost_estimate=taking(2 + width / 26),
        name="select_units",
    )(layer, to, up_b, perm, *after)


def place_kernel(slots, at_ref, *refs):
    out = refs[-1]
    for slot in range(slots):
        out[at_ref[slot]] = refs[slot][...]


def place(at, blocks, start, width, after):
    slots = len(blocks)
    features = blocks[0].shape[0]
    column = start // width
    return pl.pallas_call(
        functools.partial(place_kernel, slots),
        out_shape=jax.ShapeDtypeStruct((slots, features, width), jnp.bfloat16),
        grid_spec=pltpu.PrefetchScalarGridSpec(
            num_scalar_prefetch=1,
            grid=(1,),
            in_specs=[pl.BlockSpec((features, width), lambda i, at: (0, column))] * slots
            + [pl.BlockSpec(memory_space=pl.ANY)] * len(after),
            out_specs=pl.BlockSpec((slots, features, width), lambda i, at: (0, 0, 0)),
        ),
        compiler_params=pltpu.CompilerParams(vmem_limit_bytes=VMEM_LIMIT),
        cost_estimate=taking(1.6),
        name="place",
    )(at, *blocks, *after).reshape(slots * features, width)


def onward_kernel(odd_ref, ahead_ref, behind_ref, *refs):
    out = refs[-1]

    @pl.when(odd_ref[0] == 1)
    def _():
        out[...] = behind_ref[...]

    @pl.when(odd_ref[0] != 1)
    def _():
        out[...] = ahead_ref[...]


def onward(odd, ahead, behind, after):
    whole = pl.BlockSpec(ahead.shape, lambda i, odd: (0, 0))
    return pl.pallas_call(
        onward_kernel,
        out_shape=jax.ShapeDtypeStruct(ahead.shape, jnp.bfloat16),
        grid_spec=pltpu.PrefetchScalarGridSpec(
            num_scalar_prefetch=1,
            grid=(1,),
            in_specs=[whole, whole] + [pl.BlockSpec(memory_space=pl.ANY)] * len(after),
            out_specs=whole,
        ),
        compiler_params=pltpu.CompilerParams(vmem_limit_bytes=VMEM_LIMIT),
        cost_estimate=taking(1.6),
        name="onward",
    )(odd, ahead, behind, *after)


def pick_kernel(layer_ref, units_ref, *refs):
    refs[-1][...] = units_ref[0]


def pick(up_a, layer, after):
    _, features, units = up_a.shape
    tile = 256 if features % 256 == 0 else features
    return pl.pallas_call(
        pick_kernel,
        out_shape=jax.ShapeDtypeStruct((features, units), jnp.bfloat16),
        grid_spec=pltpu.PrefetchScalarGridSpec(
            num_scalar_prefetch=1,
            grid=(features // tile,),
            in_specs=[pl.BlockSpec((1, tile, units), lambda i, layer: (layer[0], i, 0))]
            + [pl.BlockSpec(memory_space=pl.ANY)] * len(after),
            out_specs=pl.BlockSpec((tile, units), lambda i, layer: (i, 0)),
        ),
        compiler_params=pltpu.CompilerParams(vmem_limit_bytes=VMEM_LIMIT),
        cost_estimate=taking(6.6),
        name="pick",
    )(layer, up_a, *after)


def product_kernel(blocks, joined, at_ref, *refs):
    lefts, rights = refs[: len(blocks)], refs[len(blocks) : 2 * len(blocks)]
    out = refs[-1]
    width = rights[0].shape[1]
    sums = {}
    for block, left, right in zip(blocks, lefts, rights):
        term = lax.dot_general(
            left[...], right[...], (((0,), (0,)), ((), ())), preferred_element_type=jnp.float32
        )
        start = block[1]
        sums[start] = sums[start] + term if start in sums else term
    for start, total in sums.items():
        columns = pl.ds(start, width)
        out[:, columns] = refs[2 * len(blocks)][:, columns] + total if joined else total


def product(left, at, rights, cost, offset, width, positions, joined, after):
    units = left.shape[1]
    block = rights[0][2].shape[0]
    tile = 512 if units % 512 == 0 else 256
    column = offset // width
    in_specs = [
        pl.BlockSpec((block, tile), lambda i, at, k=k: (at[k], i)) for k, _, _ in rights
    ] + [pl.BlockSpec(array.shape, lambda i, at: (0, 0)) for _, _, array in rights]
    operands = [left] * len(rights) + [array for _, _, array in rights]
    aliases = {}
    panel = pl.BlockSpec((tile, width), lambda i, at: (i, column))
    if cost is not None:
        operands.append(cost)
        in_specs.append(panel if joined else pl.BlockSpec(memory_space=pl.ANY))
        aliases = {len(operands): 0}
    operands += after
    in_specs += [pl.BlockSpec(memory_space=pl.ANY)] * len(after)
    return pl.pallas_call(
        functools.partial(product_kernel, [(k, start) for k, start, _ in rights], joined),
        out_shape=jax.ShapeDtypeStruct((units, positions), jnp.float32),
        grid_spec=pltpu.PrefetchScalarGridSpec(
            num_scalar_prefetch=1,
            grid=(units // tile,),
            in_specs=in_specs,
            out_specs=panel,
        ),
        input_output_aliases=aliases,
        compiler_params=pltpu.CompilerParams(vmem_limit_bytes=VMEM_LIMIT),
        cost_estimate=taking(11 + width / 48),
        name="product",
    )(at, *operands)


def exchange(sent, cols):
    back = [sent[0]]
    for s in range(1, cols):
        if cols & (cols - 1) == 0:
            pairs = [(i, i ^ s) for i in range(cols)]
        else:
            pairs = [(i, (i + s) % cols) for i in range(cols)]
        back.append(lax.ppermute(sent[s], "col", pairs))
    return back


def solution(mesh):
    rows, cols = mesh.shape["row"], mesh.shape["col"]
    ring = [[(i, (i + s) % rows) for i in range(rows)] for s in range(rows)]

    def shards(up_a, up_b, residual_perm, pair_index):
        r, c = lax.axis_index("row"), lax.axis_index("col")
        layer = pair_index
        positions = residual_perm.shape[0] // cols
        perm = residual_perm.reshape(cols, 1, positions)
        steps = jnp.arange(cols, dtype=jnp.int32)
        if cols & (cols - 1) == 0:
            to, come = c ^ steps, c ^ steps
        else:
            to, come = (c + steps) % cols, (c - steps) % cols
        at = (r - jnp.arange(rows, dtype=jnp.int32)) % rows
        odd = (r % 2).reshape(1).astype(jnp.int32)
        widths, order, together = plan(positions, rows)
        offsets = [sum(widths[:p]) for p in range(len(widths))]

        back, held = {}, {}
        left, cost, after = None, None, []
        for kind, number in order:
            if kind == "W":
                p, step = number.split(".")
                after = after + [held[int(p)][int(step)]]
                continue
            p = int(number)
            if kind == "S":
                members = range(p, p + together.get(p, 1))
                sent = select_units(
                    up_b, layer, perm, to, offsets[p], sum(widths[q] for q in members), after
                )
                came = exchange(sent, cols)
                for q in members:
                    back[q] = came, offsets[q] - offsets[p]
                last = sent[0]
            elif kind == "L":
                last = place(come, *back[p], widths[p], after)
                if rows == 4:
                    held[p] = [last, lax.ppermute(last, "row", ring[1]), None, lax.ppermute(last, "row", ring[3])]
                else:
                    held[p] = [last] + [lax.ppermute(last, "row", ring[s]) for s in range(1, rows)]
            elif kind == "O":
                last = onward(odd, held[p][1], held[p][3], after)
                held[p][2] = lax.ppermute(last, "row", [(0, 1), (1, 0), (2, 3), (3, 2)])
            elif kind == "A":
                last = pick(up_a, layer, after)
                left = lax.all_gather(last, "col", axis=0, tiled=True)
            else:
                rights = [(s, 0, array) for s, array in enumerate(held[p])]
                late = [array for array in after if array is not cost]
                cost = last = product(
                    left, at, rights, cost, offsets[p], widths[p], positions, False, late
                )
            after = [last]
        return cost

    placed = (
        P("groups", "col", "row"),
        P("groups", ("row", "col"), None),
        P("groups"),
        P("groups"),
    )
    return jax.shard_map(
        shards, mesh=mesh, in_specs=placed, out_specs=P(("groups", "row"), "col"), check_vma=False
    )
```

```python
import functools

import jax
import jax.numpy as jnp
from jax import lax
from jax.experimental import pallas as pl
from jax.experimental.pallas import tpu as pltpu
from jax.sharding import PartitionSpec as P

LANES = 128
VMEM_LIMIT = 52 * 2**20


def taking(us):
    return pl.CostEstimate(flops=int(us * 0.3 * 1.15e9), bytes_accessed=0, transcendentals=0)
WIDTHS = (4, 4, 4, 4, 4, 4, 2, 2)
ORDER = (
    "S0 A0 L0 S1",
    "S2 L1 O0 S3",
    "L2 O1 S4 W0.2",
    "L3 O2 S5 W1.2",
    "L4 X0 O3 S6",
    "W2.2 L5 X1 O4",
    "X2 W3.2 L6 O5",
    "X3 W4.2 O6 X4",
    "W5.2 L7 X5 O7",
    "X6 X7",
)
TOGETHER = {6: 2}


def plan(positions, rows):
    units = positions // LANES
    if sum(WIDTHS) == units and rows == 4:
        steps = " ".join(ORDER).split()
        order = [(step[0], step[1:]) for step in steps]
        return [part * LANES for part in WIDTHS], order, TOGETHER
    steps = [(kind, str(p)) for p in range(units) for kind in "SLX"]
    if rows == 4:
        steps = [(kind, str(p)) for p in range(units) for kind in "SLOX"]
    return [LANES] * units, steps[:2] + [("A", "0")] + steps[2:], {}


def select_kernel(slots, offset, layer_ref, to_ref, units_ref, perm_ref, *refs):
    outs, held = refs[-slots - 1 : -1], refs[-1]
    units = units_ref.shape[2]
    width = outs[0].shape[1]
    tile = 256 if width % 256 == 0 else width
    tiles = width // tile
    step = 1024 if units % 1024 == 0 else units

    @pl.loop(0, slots * tiles)
    def _(part):
        slot, start = part // tiles, pl.multiple_of((part % tiles) * tile, tile)
        wanted = perm_ref[to_ref[slot], :, pl.ds(pl.multiple_of(offset + start, LANES), tile)]

        total = None
        for at in range(0, units, step):
            index = lax.broadcasted_iota(jnp.int32, (step, tile), 0) + at
            hot = jnp.where(index == wanted, 1.0, 0.0).astype(jnp.bfloat16)
            term = jnp.dot(
                units_ref[0, :, at : at + step], hot, preferred_element_type=jnp.float32
            )
            total = term if total is None else total + term
        held[slot, :, pl.ds(start, tile)] = total.astype(jnp.bfloat16)

    for slot in range(slots):
        outs[slot][...] = held[slot]


def select_units(up_b, layer, perm, to, offset, width, after):
    slots, _, positions = perm.shape
    _, features, units = up_b.shape
    return pl.pallas_call(
        functools.partial(select_kernel, slots, offset),
        out_shape=[jax.ShapeDtypeStruct((features, width), jnp.bfloat16)] * slots,
        grid_spec=pltpu.PrefetchScalarGridSpec(
            num_scalar_prefetch=2,
            grid=(1,),
            in_specs=[
                pl.BlockSpec((1, features, units), lambda i, layer, to: (layer[0], 0, 0)),
                pl.BlockSpec((slots, 1, positions), lambda i, layer, to: (0, 0, 0)),
            ]
            + [pl.BlockSpec(memory_space=pl.ANY)] * len(after),
            out_specs=[pl.BlockSpec((features, width), lambda i, layer, to: (0, 0))] * slots,
            scratch_shapes=[
                pltpu.VMEM((slots, features, width), jnp.bfloat16),
            ],
        ),
        compiler_params=pltpu.CompilerParams(vmem_limit_bytes=VMEM_LIMIT),
        cost_estimate=taking(2 + width / 26),
        name="select_units",
    )(layer, to, up_b, perm, *after)


def place_kernel(slots, at_ref, *refs):
    out = refs[-1]
    for slot in range(slots):
        out[at_ref[slot]] = refs[slot][...]


def place(at, blocks, start, width, after):
    slots = len(blocks)
    features = blocks[0].shape[0]
    column = start // width
    return pl.pallas_call(
        functools.partial(place_kernel, slots),
        out_shape=jax.ShapeDtypeStruct((slots, features, width), jnp.bfloat16),
        grid_spec=pltpu.PrefetchScalarGridSpec(
            num_scalar_prefetch=1,
            grid=(1,),
            in_specs=[pl.BlockSpec((features, width), lambda i, at: (0, column))] * slots
            + [pl.BlockSpec(memory_space=pl.ANY)] * len(after),
            out_specs=pl.BlockSpec((slots, features, width), lambda i, at: (0, 0, 0)),
        ),
        compiler_params=pltpu.CompilerParams(vmem_limit_bytes=VMEM_LIMIT),
        cost_estimate=taking(1.6),
        name="place",
    )(at, *blocks, *after).reshape(slots * features, width)


def onward_kernel(odd_ref, ahead_ref, behind_ref, *refs):
    out = refs[-1]

    @pl.when(odd_ref[0] == 1)
    def _():
        out[...] = behind_ref[...]

    @pl.when(odd_ref[0] != 1)
    def _():
        out[...] = ahead_ref[...]


def onward(odd, ahead, behind, after):
    whole = pl.BlockSpec(ahead.shape, lambda i, odd: (0, 0))
    return pl.pallas_call(
        onward_kernel,
        out_shape=jax.ShapeDtypeStruct(ahead.shape, jnp.bfloat16),
        grid_spec=pltpu.PrefetchScalarGridSpec(
            num_scalar_prefetch=1,
            grid=(1,),
            in_specs=[whole, whole] + [pl.BlockSpec(memory_space=pl.ANY)] * len(after),
            out_specs=whole,
        ),
        compiler_params=pltpu.CompilerParams(vmem_limit_bytes=VMEM_LIMIT),
        cost_estimate=taking(1.6),
        name="onward",
    )(odd, ahead, behind, *after)


def pick_kernel(layer_ref, units_ref, *refs):
    refs[-1][...] = units_ref[0]


def pick(up_a, layer, after):
    _, features, units = up_a.shape
    tile = 256 if features % 256 == 0 else features
    return pl.pallas_call(
        pick_kernel,
        out_shape=jax.ShapeDtypeStruct((features, units), jnp.bfloat16),
        grid_spec=pltpu.PrefetchScalarGridSpec(
            num_scalar_prefetch=1,
            grid=(features // tile,),
            in_specs=[pl.BlockSpec((1, tile, units), lambda i, layer: (layer[0], i, 0))]
            + [pl.BlockSpec(memory_space=pl.ANY)] * len(after),
            out_specs=pl.BlockSpec((tile, units), lambda i, layer: (i, 0)),
        ),
        compiler_params=pltpu.CompilerParams(vmem_limit_bytes=VMEM_LIMIT),
        cost_estimate=taking(6.6),
        name="pick",
    )(layer, up_a, *after)


def product_kernel(blocks, joined, at_ref, *refs):
    lefts, rights = refs[: len(blocks)], refs[len(blocks) : 2 * len(blocks)]
    out = refs[-1]
    width = rights[0].shape[1]
    sums = {}
    for block, left, right in zip(blocks, lefts, rights):
        term = lax.dot_general(
            left[...], right[...], (((0,), (0,)), ((), ())), preferred_element_type=jnp.float32
        )
        start = block[1]
        sums[start] = sums[start] + term if start in sums else term
    for start, total in sums.items():
        columns = pl.ds(start, width)
        out[:, columns] = refs[2 * len(blocks)][:, columns] + total if joined else total


def product(left, at, rights, cost, offset, width, positions, joined, after):
    units = left.shape[1]
    block = rights[0][2].shape[0]
    tile = 896 if units % 896 == 0 else 256
    column = offset // width
    in_specs = [
        pl.BlockSpec((block, tile), lambda i, at, k=k: (at[k], i)) for k, _, _ in rights
    ] + [pl.BlockSpec(array.shape, lambda i, at: (0, 0)) for _, _, array in rights]
    operands = [left] * len(rights) + [array for _, _, array in rights]
    aliases = {}
    panel = pl.BlockSpec((tile, width), lambda i, at: (i, column))
    if cost is not None:
        operands.append(cost)
        in_specs.append(panel if joined else pl.BlockSpec(memory_space=pl.ANY))
        aliases = {len(operands): 0}
    operands += after
    in_specs += [pl.BlockSpec(memory_space=pl.ANY)] * len(after)
    return pl.pallas_call(
        functools.partial(product_kernel, [(k, start) for k, start, _ in rights], joined),
        out_shape=jax.ShapeDtypeStruct((units, positions), jnp.float32),
        grid_spec=pltpu.PrefetchScalarGridSpec(
            num_scalar_prefetch=1,
            grid=(units // tile,),
            in_specs=in_specs,
            out_specs=panel,
        ),
        input_output_aliases=aliases,
        compiler_params=pltpu.CompilerParams(vmem_limit_bytes=VMEM_LIMIT),
        cost_estimate=taking(11 + width / 48),
        name="product",
    )(at, *operands)


def exchange(sent, cols):
    back = [sent[0]]
    for s in range(1, cols):
        if cols & (cols - 1) == 0:
            pairs = [(i, i ^ s) for i in range(cols)]
        else:
            pairs = [(i, (i + s) % cols) for i in range(cols)]
        back.append(lax.ppermute(sent[s], "col", pairs))
    return back


def solution(mesh):
    rows, cols = mesh.shape["row"], mesh.shape["col"]
    ring = [[(i, (i + s) % rows) for i in range(rows)] for s in range(rows)]

    def shards(up_a, up_b, residual_perm, pair_index):
        r, c = lax.axis_index("row"), lax.axis_index("col")
        layer = pair_index
        positions = residual_perm.shape[0] // cols
        perm = residual_perm.reshape(cols, 1, positions)
        steps = jnp.arange(cols, dtype=jnp.int32)
        if cols & (cols - 1) == 0:
            to, come = c ^ steps, c ^ steps
        else:
            to, come = (c + steps) % cols, (c - steps) % cols
        at = (r - jnp.arange(rows, dtype=jnp.int32)) % rows
        odd = (r % 2).reshape(1).astype(jnp.int32)
        widths, order, together = plan(positions, rows)
        offsets = [sum(widths[:p]) for p in range(len(widths))]

        back, held = {}, {}
        left, cost, after = None, None, []
        for kind, number in order:
            if kind == "W":
                p, step = number.split(".")
                after = after + [held[int(p)][int(step)]]
                continue
            p = int(number)
            if kind == "S":
                members = range(p, p + together.get(p, 1))
                sent = select_units(
                    up_b, layer, perm, to, offsets[p], sum(widths[q] for q in members), after
                )
                came = exchange(sent, cols)
                for q in members:
                    back[q] = came, offsets[q] - offsets[p]
                last = sent[0]
            elif kind == "L":
                last = place(come, *back[p], widths[p], after)
                if rows == 4:
                    held[p] = [last, lax.ppermute(last, "row", ring[1]), None, lax.ppermute(last, "row", ring[3])]
                else:
                    held[p] = [last] + [lax.ppermute(last, "row", ring[s]) for s in range(1, rows)]
            elif kind == "O":
                last = onward(odd, held[p][1], held[p][3], after)
                held[p][2] = lax.ppermute(last, "row", [(0, 1), (1, 0), (2, 3), (3, 2)])
            elif kind == "A":
                last = pick(up_a, layer, after)
                left = lax.all_gather(last, "col", axis=0, tiled=True)
            else:
                rights = [(s, 0, array) for s, array in enumerate(held[p])]
                late = [array for array in after if array is not cost]
                cost = last = product(
                    left, at, rights, cost, offsets[p], widths[p], positions, False, late
                )
            after = [last]
        return cost

    placed = (
        P("groups", "col", "row"),
        P("groups", ("row", "col"), None),
        P("groups"),
        P("groups"),
    )
    return jax.shard_map(
        shards, mesh=mesh, in_specs=placed, out_specs=P(("groups", "row"), "col"), check_vma=False
    )
```
